32 devices in a mesh: depth: 4 (over y, x), tile: 8 (over z, core).
Axes of the slice: x: 2, y: 2, z: 4, core: 2. Of those that a mesh axis runs over, the one named last changes fastest.
Arguments:
- density: float32 [128, 256, 2048], P('depth', 'tile'), may hold values from 0 to 1
- palette: float32 [2, 3], replicated, may hold values from 0.2 to 1
- light_dir: float32 [2, 3], replicated, may hold values from -4 to 4
- slab_of: int32 [4], replicated, may hold values from 0 to 3, each once
Outputs:
- images: float32 [2, 4, 256, 2048], P(None, None, 'tile', 'depth')
The draws below stay inside these ranges and needn't reach their ends.
Inputs may be any that keep to these rules, and one draw needn't show every extreme that they name: `slab_of`: each of 0 to 3 appears once.
All inputs are finite; a program needn't handle non-finite values.
Results may differ from the reference program's by a relative error of at most 0.0008.
Values may be sent and summed in bfloat16 or wider, within the bound.
A program may use at most 128 MiB of HBM per device.

```python
import jax
import jax.numpy as jnp
from jax import lax

CZ = 32
NX = 256
NY = 2048
NZ = 128
N_DEPTH = 4


def level_of(rng, shape, pieces, least, largest):
    factor_of, own = 1.0, jax.random.fold_in(rng, 6)
    for axis_at, shards_of in pieces:
        heights = jnp.exp(jax.random.uniform(jax.random.fold_in(own, axis_at), (shards_of,), jnp.float32, least / len(pieces), largest / len(pieces)))
        factor_of = factor_of * jnp.repeat(heights, shape[axis_at] // shards_of).reshape([-1 if axis == axis_at else 1 for axis in range(len(shape))])
    return factor_of


def scatter_about(own_key, shape, deviation, bound, kind=jnp.bfloat16):
    values = jax.random.normal(own_key, shape, jnp.float32) * deviation
    return jnp.minimum(jnp.maximum(values, -bound), bound).astype(kind)


def setup_inputs(seed: int = 0) -> dict:
    streams_of = jax.random.split(jax.random.key(seed), 5)
    density = jnp.clip(1.0 * jax.random.uniform(streams_of[0], (NZ, NX, NY), jnp.float32) ** level_of(streams_of[0], (NZ, NX, NY), ((0, 4), (1, 8)), -0.2, 0.2), 0.0, 1.0)
    palette = jnp.clip(jax.random.uniform(streams_of[1], (2, 3), jnp.float32, 0.2, 1.0), 0.2, 1.0)
    light_dir = scatter_about(streams_of[2], (2, 3), 1.0, 4.0, jnp.float32)
    slab_of = jax.random.permutation(streams_of[3], N_DEPTH).astype(jnp.int32)
    return dict(density=density, palette=palette, light_dir=light_dir, slab_of=slab_of)


HIGH = lax.Precision.HIGHEST

def centred(field, axis):
    size = field.shape[axis]
    upper = jnp.concatenate([lax.slice_in_dim(field, 1, size, axis=axis), lax.slice_in_dim(field, size - 1, size, axis=axis)], axis)
    lower = jnp.concatenate([lax.slice_in_dim(field, 0, 1, axis=axis), lax.slice_in_dim(field, 0, size - 1, axis=axis)], axis)
    return (upper - lower) * 0.5

def march(block, grad_x, palette, light_dir, factor):
    grad_z = centred(block, 0)
    grad_y = centred(block, 2)
    length = jnp.sqrt(grad_x * grad_x + grad_y * grad_y + grad_z * grad_z + 0.25)
    optical = block * factor
    opacity = 1.0 - jnp.exp(-optical)
    running = jnp.cumsum(optical, axis=0)
    slab_tau = running[-1]
    before = [running - optical, slab_tau[None] - running]
    colours = []
    for view in range(2):
        facing = grad_x * light_dir[view, 0] + grad_y * light_dir[view, 1] + grad_z * light_dir[view, 2]
        shade = 0.3 + jnp.abs(facing) / length
        weight = opacity * jnp.exp(-before[view]) * shade
        plain = lax.optimization_barrier(jnp.sum(weight, axis=0))
        dense = lax.optimization_barrier(jnp.sum(block * weight, axis=0))
        colours.append(palette[0][:, None, None] * plain[None] + palette[1][:, None, None] * dense[None])
    return (jnp.stack(colours).astype(jnp.bfloat16), slab_tau.astype(jnp.bfloat16))

def compose(slab_rgb, slab_tau, slab_of):
    tau_full = slab_tau.astype(jnp.float32)
    earlier = (slab_of[None, :] < slab_of[:, None]).astype(jnp.float32)
    later = (slab_of[None, :] > slab_of[:, None]).astype(jnp.float32)
    front_one = jnp.einsum('jk,kxy->jxy', earlier, tau_full, precision=HIGH)
    front_two = jnp.einsum('jk,kxy->jxy', later, tau_full, precision=HIGH)
    rgb_full = slab_rgb.astype(jnp.float32)
    colour_one = jnp.einsum('jcxy,jxy->cxy', rgb_full[:, 0], jnp.exp(-front_one), precision=HIGH)
    colour_two = jnp.einsum('jcxy,jxy->cxy', rgb_full[:, 1], jnp.exp(-front_two), precision=HIGH)
    coverage = 1.0 - jnp.exp(-lax.optimization_barrier(jnp.sum(tau_full, axis=0)))
    return jnp.stack([jnp.concatenate([colour_one, coverage[None]], 0), jnp.concatenate([colour_two, coverage[None]], 0)])

def reference(density, palette, light_dir, slab_of):
    factor = 3.0 / NZ

    def one_block(index):
        block = lax.dynamic_slice_in_dim(density, index * CZ, CZ, 0)
        return march(block, centred(block, 1), palette, light_dir, factor)
    slab_rgb, slab_tau = lax.map(one_block, jnp.arange(N_DEPTH, dtype=jnp.int32))
    return compose(slab_rgb, slab_tau, slab_of)
```

```python
import functools
import math

import jax
import jax.numpy as jnp
from jax import lax
from jax.experimental import pallas as pl
from jax.experimental.pallas import tpu as pltpu
from jax.sharding import PartitionSpec as P

LANES = 128
SUB = 8
UNIT = 16
PAD = 8


def partner(me, step, count):
    if count & (count - 1):
        return lax.rem(me + step, count)
    out, bit = 0, 1
    while bit < count:
        mine = lax.rem(me // bit, 2)
        out = out + bit * (1 - mine if step & bit else mine)
        bit *= 2
    return out


def kernel(
    geom, density, palette, light, slab_of, out, buf, stag, send, recv,
    load_sem, halo_send, halo_recv, send_sem, recv_sem,
):
    rows, xs, ncols, depth_n, tile_n, tiles_per, group, unroll = geom
    tiles = ncols // LANES
    me = lax.axis_index("depth")
    tile = lax.axis_index("tile")
    left = lax.rem(tile + tile_n - 1, tile_n)
    right = lax.rem(tile + 1, tile_n)
    barrier = pltpu.get_barrier_semaphore()
    for step in range(1, depth_n):
        pl.semaphore_signal(
            barrier, inc=1, device_id={"depth": partner(me, step, depth_n)},
            device_id_type=pl.DeviceIdType.MESH,
        )
    for side in (left, right):
        pl.semaphore_signal(
            barrier, inc=1, device_id={"tile": side}, device_id_type=pl.DeviceIdType.MESH
        )

    def load(j):
        return pltpu.make_async_copy(
            density.at[:, :, pl.ds(j * LANES, LANES)],
            buf.at[:, j, pl.ds(PAD, xs), :],
            load_sem.at[j],
        )

    for j in range(tiles):
        load(j).start()
    pl.semaphore_wait(barrier, depth_n + 1)

    low_row, high_row = PAD - 1, PAD + xs

    def halo_to(j, side, target):
        source, row = ((xs - 1, low_row), (0, high_row))[side]
        return pltpu.make_async_remote_copy(
            src_ref=density.at[:, pl.ds(source, 1), pl.ds(j * LANES, LANES)],
            dst_ref=buf.at[:, j, pl.ds(row, 1), :],
            send_sem=halo_send.at[side, j],
            recv_sem=halo_recv.at[side, j],
            device_id={"tile": target},
            device_id_type=pl.DeviceIdType.MESH,
        )

    def halo_own(j, side):
        source, row = ((0, low_row), (xs - 1, high_row))[side]
        return pltpu.make_async_copy(
            density.at[:, pl.ds(source, 1), pl.ds(j * LANES, LANES)],
            buf.at[:, j, pl.ds(row, 1), :],
            halo_recv.at[side, j],
        )

    @pl.when(tile < tile_n - 1)
    def _():
        for j in range(tiles):
            halo_to(j, 0, right).start()

    @pl.when(tile > 0)
    def _():
        for j in range(tiles):
            halo_to(j, 1, left).start()

    @pl.when(tile == 0)
    def _():
        for j in range(tiles):
            halo_own(j, 0).start()

    @pl.when(tile == tile_n - 1)
    def _():
        for j in range(tiles):
            halo_own(j, 1).start()

    for j in range(tiles):
        load(j).wait()

    factor = 3.0 / (rows * depth_n)
    scale = factor * math.log2(math.e)
    lights = [[light[v, c] for c in range(3)] for v in range(2)]
    colours = [[palette[a, c] for c in range(3)] for a in range(2)]
    lane = lax.broadcasted_iota(jnp.int32, (group, SUB, LANES), 2)
    place = lax.broadcasted_iota(jnp.int32, (group, SUB, LANES), 0)
    first, last = lane == 0, lane == LANES - 1

    def sweep(j0, x0, stag_j, stag_row):
        end_low = first & (place == 0) & (j0 == 0)
        end_high = last & (place == group - 1) & (j0 + group == tiles)
        j_low = jnp.maximum(j0 - 1, 0)
        j_high = jnp.minimum(j0 + group, tiles - 1)
        here = pl.ds(pl.multiple_of(x0 + PAD, SUB), SUB)

        def at(z, offset=0):
            return buf[z, pl.ds(j0, group), pl.ds(x0 + PAD + offset, SUB), :]

        def block(step, carry):
            run, seen, grown, p0, d0, p1, d1 = carry
            z0 = step * unroll
            below = at(jnp.maximum(z0 - 1, 0))
            mid = at(z0)
            for i in range(unroll):
                z = z0 + i
                above = at(jnp.minimum(z + 1, rows - 1) if i == unroll - 1 else z + 1)
                gz = above - below
                gx = at(z, 1) - at(z, -1)
                edge_low = buf[z, pl.ds(j_low, 1), here, :]
                edge_high = buf[z, pl.ds(j_high, 1), here, :]
                if group > 1:
                    edge_low = jnp.concatenate([edge_low, mid[:-1]], 0)
                    edge_high = jnp.concatenate([mid[1:], edge_high], 0)
                prior = pltpu.roll(jnp.where(last, edge_low, mid), 1, 2)
                after = pltpu.roll(jnp.where(first, edge_high, mid), LANES - 1, 2)
                prior = jnp.where(end_low, mid, prior)
                after = jnp.where(end_high, mid, after)
                gy = after - prior
                inverse = lax.rsqrt(gx * gx + gy * gy + (gz * gz + 1.0))
                shades = [
                    jnp.abs(gx * l[0] + gy * l[1] + gz * l[2]) * inverse + 0.3 for l in lights
                ]
                run = run + mid
                power = run * scale
                seen_next = jnp.exp2(-power)
                grown_next = jnp.exp2(power)
                c0 = (seen - seen_next) * shades[0]
                c1 = (grown_next - grown) * shades[1]
                p0 = p0 + c0
                d0 = d0 + mid * c0
                p1 = p1 + c1
                d1 = d1 + mid * c1
                seen, grown = seen_next, grown_next
                below, mid = mid, above
            return run, seen, grown, p0, d0, p1, d1

        zero = jnp.zeros((group, SUB, LANES), jnp.float32)
        one = jnp.ones((group, SUB, LANES), jnp.float32)
        run, seen, _, p0, d0, p1, d1 = lax.fori_loop(
            0, rows // unroll, block, (zero, one, one, zero, zero, zero, zero)
        )
        p1, d1 = p1 * seen, d1 * seen
        fields = [colours[0][c] * p0 + colours[1][c] * d0 for c in range(3)]
        fields += [colours[0][c] * p1 + colours[1][c] * d1 for c in range(3)]
        fields.append(run * factor)
        for f, value in enumerate(fields):
            stag[f, pl.ds(stag_j, group), pl.ds(pl.multiple_of(stag_row, SUB), SUB), :] = value

    groups = tiles_per // group

    def unit(dest, x_first, x_step, target):
        def part(index, _):
            half, piece = index // groups, lax.rem(index, groups)
            sweep(
                dest * tiles_per + piece * group, x_first + half * x_step, piece * group, half * SUB
            )
            return 0

        lax.fori_loop(0, 2 * groups, part, 0)
        for f in range(7):
            for j in range(tiles_per):
                target[f, :, pl.ds(j * LANES, LANES)] = stag[f, j].astype(jnp.bfloat16)

    def outgoing(step, u):
        return pltpu.make_async_remote_copy(
            src_ref=send.at[step - 1, u],
            dst_ref=recv.at[me, u],
            send_sem=send_sem.at[step - 1, u],
            recv_sem=recv_sem.at[me, u],
            device_id={"depth": partner(me, step, depth_n)},
            device_id_type=pl.DeviceIdType.MESH,
        )

    def incoming(source, u):
        return pltpu.make_async_remote_copy(
            src_ref=send.at[0, u],
            dst_ref=recv.at[source, u],
            send_sem=send_sem.at[0, u],
            recv_sem=recv_sem.at[source, u],
            device_id={"depth": source},
            device_id_type=pl.DeviceIdType.MESH,
        )

    pairs = xs // UNIT
    for u in range(pairs):
        if u == pairs - 1:
            for j in range(tiles):
                for side, has in ((0, tile > 0), (1, tile < tile_n - 1)):

                    @pl.when(has)
                    def _(j=j, side=side):
                        halo_to(j, side, (right, left)[side]).wait_recv()

                    @pl.when(jnp.logical_not(has))
                    def _(j=j, side=side):
                        halo_own(j, side).wait()

        if u == pairs - 1:
            x_first, x_step = 0, xs - SUB
        else:
            x_first, x_step = SUB + u * UNIT, SUB
        for step in range(depth_n - 1, 0, -1):
            unit(partner(me, step, depth_n), x_first, x_step, send.at[step - 1, u])
            outgoing(step, u).start()
        unit(me, x_first, x_step, recv.at[me, u])

    order = [slab_of[k] for k in range(depth_n)]
    for u in range(pairs):
        for step in range(1, depth_n):
            incoming(partner(me, step, depth_n), u).wait_recv()
        if u == pairs - 1:
            x_first, x_step = 0, xs - SUB
        else:
            x_first, x_step = SUB + u * UNIT, SUB

        def compose(j, _):
            cols = pl.ds(pl.multiple_of(j * LANES, LANES), LANES)
            taus = [recv[k, u, 6, :, cols].astype(jnp.float32) for k in range(depth_n)]
            total = functools.reduce(jnp.add, taus)
            coverage = 1.0 - jnp.exp(-total)
            sums = [[0.0] * 3 for _ in range(2)]
            for b in range(depth_n):
                front = jnp.zeros_like(total)
                behind = jnp.zeros_like(total)
                for k in range(depth_n):
                    if k != b:
                        front += jnp.where(order[k] < order[b], 1.0, 0.0) * taus[k]
                        behind += jnp.where(order[k] > order[b], 1.0, 0.0) * taus[k]
                for v, depth in enumerate((front, behind)):
                    fade = jnp.exp(-depth)
                    for c in range(3):
                        value = recv[b, u, 3 * v + c, :, cols].astype(jnp.float32)
                        sums[v][c] = sums[v][c] + value * fade
            for v in range(2):
                for c, value in enumerate(sums[v] + [coverage]):
                    for half in range(2):
                        out[v, c, pl.ds(x_first + half * x_step, SUB), cols] = value[
                            half * SUB : (half + 1) * SUB
                        ]
            return 0

        lax.fori_loop(0, tiles_per, compose, 0)

    for u in range(pairs):
        for step in range(1, depth_n):
            outgoing(step, u).wait_send()
    for j in range(tiles):

        @pl.when(tile < tile_n - 1)
        def _(j=j):
            halo_to(j, 0, right).wait_send()

        @pl.when(tile > 0)
        def _(j=j):
            halo_to(j, 1, left).wait_send()


def on_device(depth_n, tile_n, density, palette, light_dir, slab_of):
    rows, xs, ncols = density.shape
    tiles = ncols // LANES
    tiles_per = tiles // depth_n
    group = 2 if tiles_per % 2 == 0 else 1
    unroll = 16
    geom = (rows, xs, ncols, depth_n, tile_n, tiles_per, group, unroll)
    pairs = xs // UNIT
    cols = ncols // depth_n
    smem = pl.BlockSpec(memory_space=pltpu.SMEM)
    return pl.pallas_call(
        functools.partial(kernel, geom),
        out_shape=jax.ShapeDtypeStruct((2, 4, xs, cols), jnp.float32),
        in_specs=[pl.BlockSpec(memory_space=pl.ANY), smem, smem, smem],
        out_specs=pl.BlockSpec(memory_space=pltpu.VMEM),
        scratch_shapes=[
            pltpu.VMEM((rows, tiles, xs + 2 * PAD, LANES), jnp.float32),
            pltpu.VMEM((7, tiles_per, UNIT, LANES), jnp.float32),
            pltpu.VMEM((depth_n - 1, pairs, 7, UNIT, cols), jnp.bfloat16),
            pltpu.VMEM((depth_n, pairs, 7, UNIT, cols), jnp.bfloat16),
            pltpu.SemaphoreType.DMA((tiles,)),
            pltpu.SemaphoreType.DMA((2, tiles)),
            pltpu.SemaphoreType.DMA((2, tiles)),
            pltpu.SemaphoreType.DMA((depth_n - 1, pairs)),
            pltpu.SemaphoreType.DMA((depth_n, pairs)),
        ],
        compiler_params=pltpu.CompilerParams(
            collective_id=0, has_side_effects=True, vmem_limit_bytes=40 * 1024 * 1024
        ),
        name="render",
    )(density, palette, light_dir, slab_of)


def solution(mesh):
    in_specs = (P("depth", "tile", None), P(), P(), P())
    out_specs = P(None, None, "tile", "depth")
    body = functools.partial(on_device, mesh.shape["depth"], mesh.shape["tile"])
    return jax.shard_map(
        body, mesh=mesh, in_specs=in_specs, out_specs=out_specs, check_vma=False
    )
```

```python
import functools
import math

import jax
import jax.numpy as jnp
from jax import lax
from jax.experimental import pallas as pl
from jax.experimental.pallas import tpu as pltpu
from jax.sharding import PartitionSpec as P

LANES = 128
SUB = 8
UNIT = 16
PAD = 8


def partner(me, step, count):
    if count & (count - 1):
        return lax.rem(me + step, count)
    out, bit = 0, 1
    while bit < count:
        mine = lax.rem(me // bit, 2)
        out = out + bit * (1 - mine if step & bit else mine)
        bit *= 2
    return out


def kernel(
    geom, density, palette, light, slab_of, out, buf, stag, send, recv,
    load_sem, halo_send, halo_recv, send_sem, recv_sem,
):
    rows, xs, ncols, depth_n, tile_n, tiles_per, group, unroll = geom
    tiles = ncols // LANES
    me = lax.axis_index("depth")
    tile = lax.axis_index("tile")
    left = lax.rem(tile + tile_n - 1, tile_n)
    right = lax.rem(tile + 1, tile_n)
    barrier = pltpu.get_barrier_semaphore()
    for step in range(1, depth_n):
        pl.semaphore_signal(
            barrier, inc=1, device_id={"depth": partner(me, step, depth_n)},
            device_id_type=pl.DeviceIdType.MESH,
        )
    for side in (left, right):
        pl.semaphore_signal(
            barrier, inc=1, device_id={"tile": side}, device_id_type=pl.DeviceIdType.MESH
        )

    def load(j):
        return pltpu.make_async_copy(
            density.at[:, :, pl.ds(j * LANES, LANES)],
            buf.at[:, j + 1, pl.ds(PAD, xs), :],
            load_sem.at[j],
        )

    for j in range(tiles):
        load(j).start()
    pl.semaphore_wait(barrier, depth_n + 1)

    low_row, high_row = PAD - 1, PAD + xs

    def halo_to(j, side, target):
        source, row = ((xs - 1, low_row), (0, high_row))[side]
        return pltpu.make_async_remote_copy(
            src_ref=density.at[:, pl.ds(source, 1), pl.ds(j * LANES, LANES)],
            dst_ref=buf.at[:, j + 1, pl.ds(row, 1), :],
            send_sem=halo_send.at[side, j],
            recv_sem=halo_recv.at[side, j],
            device_id={"tile": target},
            device_id_type=pl.DeviceIdType.MESH,
        )

    def halo_own(j, side):
        source, row = ((0, low_row), (xs - 1, high_row))[side]
        return pltpu.make_async_copy(
            density.at[:, pl.ds(source, 1), pl.ds(j * LANES, LANES)],
            buf.at[:, j + 1, pl.ds(row, 1), :],
            halo_recv.at[side, j],
        )

    @pl.when(tile < tile_n - 1)
    def _():
        for j in range(tiles):
            halo_to(j, 0, right).start()

    @pl.when(tile > 0)
    def _():
        for j in range(tiles):
            halo_to(j, 1, left).start()

    @pl.when(tile == 0)
    def _():
        for j in range(tiles):
            halo_own(j, 0).start()

    @pl.when(tile == tile_n - 1)
    def _():
        for j in range(tiles):
            halo_own(j, 1).start()

    for j in range(tiles):
        load(j).wait()

    def pad_columns(z, _):
        for x0 in range(0, xs, SUB):
            here = pl.ds(PAD + x0, SUB)
            buf[z, 0, here, :] = pltpu.roll(buf[z, 1, here, :], LANES - 1, 1)
            buf[z, tiles + 1, here, :] = pltpu.roll(buf[z, tiles, here, :], 1, 1)
        return 0

    lax.fori_loop(0, rows, pad_columns, 0, unroll=4)

    factor = 3.0 / (rows * depth_n)
    scale = factor * math.log2(math.e)
    lights = [[light[v, c] for c in range(3)] for v in range(2)]
    colours = [[palette[a, c] for c in range(3)] for a in range(2)]
    lane = lax.broadcasted_iota(jnp.int32, (group, SUB, LANES), 2)
    first, last = lane == 0, lane == LANES - 1

    def sweep(j0, x0, stag_j, stag_row):
        here = pl.ds(pl.multiple_of(x0 + PAD, SUB), SUB)

        def at(z, offset=0):
            where = pl.ds(x0 + PAD + offset, SUB) if offset else here
            return buf[z, pl.ds(j0 + 1, group), where, :]

        def block(step, carry):
            run, seen, grown, p0, d0, p1, d1 = carry
            z0 = step * unroll
            below = at(max(z0 - 1, 0) if unroll == rows else jnp.maximum(z0 - 1, 0))
            mid = at(z0)
            for i in range(unroll):
                z = z0 + i
                if unroll == rows:
                    above = at(min(z + 1, rows - 1))
                else:
                    above = at(jnp.minimum(z + 1, rows - 1) if i == unroll - 1 else z + 1)
                gz = above - below
                gx = at(z, 1) - at(z, -1)
                edge_low = buf[z, pl.ds(j0, 1), here, :]
                edge_high = buf[z, pl.ds(j0 + group + 1, 1), here, :]
                if group > 1:
                    edge_low = jnp.concatenate([edge_low, mid[:-1]], 0)
                    edge_high = jnp.concatenate([mid[1:], edge_high], 0)
                prior = pltpu.roll(jnp.where(last, edge_low, mid), 1, 2)
                after = pltpu.roll(jnp.where(first, edge_high, mid), LANES - 1, 2)
                gy = after - prior
                inverse = lax.rsqrt(gx * gx + gy * gy + (gz * gz + 1.0))
                shades = [
                    jnp.abs(gx * l[0] + gy * l[1] + gz * l[2]) * inverse + 0.3 for l in lights
                ]
                run = run + mid
                power = run * scale
                seen_next = jnp.exp2(-power)
                grown_next = jnp.exp2(power)
                c0 = (seen - seen_next) * shades[0]
                c1 = (grown_next - grown) * shades[1]
                p0 = p0 + c0
                d0 = d0 + mid * c0
                p1 = p1 + c1
                d1 = d1 + mid * c1
                seen, grown = seen_next, grown_next
                below, mid = mid, above
            return run, seen, grown, p0, d0, p1, d1

        zero = jnp.zeros((group, SUB, LANES), jnp.float32)
        one = jnp.ones((group, SUB, LANES), jnp.float32)
        carry = (zero, one, one, zero, zero, zero, zero)
        if unroll == rows:
            carry = block(0, carry)
        else:
            carry = lax.fori_loop(0, rows // unroll, block, carry)
        run, seen, _, p0, d0, p1, d1 = carry
        p1, d1 = p1 * seen, d1 * seen
        fields = [colours[0][c] * p0 + colours[1][c] * d0 for c in range(3)]
        fields += [colours[0][c] * p1 + colours[1][c] * d1 for c in range(3)]
        fields.append(run * factor)
        for f, value in enumerate(fields):
            stag[f, pl.ds(stag_j, group), pl.ds(pl.multiple_of(stag_row, SUB), SUB), :] = value

    groups = tiles_per // group

    def unit(dest, x_first, x_step, target):
        def part(index, _):
            half, piece = index // groups, lax.rem(index, groups)
            sweep(
                dest * tiles_per + piece * group, x_first + half * x_step, piece * group, half * SUB
            )
            return 0

        lax.fori_loop(0, 2 * groups, part, 0)
        for f in range(7):
            for j in range(tiles_per):
                target[f, :, pl.ds(j * LANES, LANES)] = stag[f, j].astype(jnp.bfloat16)

    def outgoing(step, u):
        return pltpu.make_async_remote_copy(
            src_ref=send.at[step - 1, u],
            dst_ref=recv.at[me, u],
            send_sem=send_sem.at[step - 1, u],
            recv_sem=recv_sem.at[me, u],
            device_id={"depth": partner(me, step, depth_n)},
            device_id_type=pl.DeviceIdType.MESH,
        )

    def incoming(source, u):
        return pltpu.make_async_remote_copy(
            src_ref=send.at[0, u],
            dst_ref=recv.at[source, u],
            send_sem=send_sem.at[0, u],
            recv_sem=recv_sem.at[source, u],
            device_id={"depth": source},
            device_id_type=pl.DeviceIdType.MESH,
        )

    pairs = xs // UNIT

    def rows_of(u):
        return (0, xs - SUB) if u == pairs - 1 else (SUB + u * UNIT, SUB)

    for u in range(pairs):
        if u == pairs - 1:
            for j in range(tiles):
                for side, has in ((0, tile > 0), (1, tile < tile_n - 1)):

                    @pl.when(has)
                    def _(j=j, side=side):
                        halo_to(j, side, (right, left)[side]).wait_recv()

                    @pl.when(jnp.logical_not(has))
                    def _(j=j, side=side):
                        halo_own(j, side).wait()

        for step in range(depth_n - 1, 0, -1):
            unit(partner(me, step, depth_n), *rows_of(u), send.at[step - 1, u])
            outgoing(step, u).start()

    for u in range(pairs):
        unit(me, *rows_of(u), recv.at[me, u])

    order = [slab_of[k] for k in range(depth_n)]
    for u in range(pairs):
        for step in range(1, depth_n):
            incoming(partner(me, step, depth_n), u).wait_recv()
        x_first, x_step = rows_of(u)

        def compose(j, _):
            cols = pl.ds(pl.multiple_of(j * LANES, LANES), LANES)
            taus = [recv[k, u, 6, :, cols].astype(jnp.float32) for k in range(depth_n)]
            total = functools.reduce(jnp.add, taus)
            coverage = 1.0 - jnp.exp(-total)
            sums = [[0.0] * 3 for _ in range(2)]
            for b in range(depth_n):
                front = jnp.zeros_like(total)
                behind = jnp.zeros_like(total)
                for k in range(depth_n):
                    if k != b:
                        front += jnp.where(order[k] < order[b], 1.0, 0.0) * taus[k]
                        behind += jnp.where(order[k] > order[b], 1.0, 0.0) * taus[k]
                for v, depth in enumerate((front, behind)):
                    fade = jnp.exp(-depth)
                    for c in range(3):
                        value = recv[b, u, 3 * v + c, :, cols].astype(jnp.float32)
                        sums[v][c] = sums[v][c] + value * fade
            for v in range(2):
                for c, value in enumerate(sums[v] + [coverage]):
                    for half in range(2):
                        out[v, c, pl.ds(x_first + half * x_step, SUB), cols] = value[
                            half * SUB : (half + 1) * SUB
                        ]
            return 0

        lax.fori_loop(0, tiles_per, compose, 0)

    for u in range(pairs):
        for step in range(1, depth_n):
            outgoing(step, u).wait_send()
    for j in range(tiles):

        @pl.when(tile < tile_n - 1)
        def _(j=j):
            halo_to(j, 0, right).wait_send()

        @pl.when(tile > 0)
        def _(j=j):
            halo_to(j, 1, left).wait_send()


def on_device(depth_n, tile_n, density, palette, light_dir, slab_of):
    rows, xs, ncols = density.shape
    tiles = ncols // LANES
    tiles_per = tiles // depth_n
    group = 2 if tiles_per % 2 == 0 else 1
    unroll = rows
    geom = (rows, xs, ncols, depth_n, tile_n, tiles_per, group, unroll)
    pairs = xs // UNIT
    cols = ncols // depth_n
    smem = pl.BlockSpec(memory_space=pltpu.SMEM)
    return pl.pallas_call(
        functools.partial(kernel, geom),
        out_shape=jax.ShapeDtypeStruct((2, 4, xs, cols), jnp.float32),
        in_specs=[pl.BlockSpec(memory_space=pl.ANY), smem, smem, smem],
        out_specs=pl.BlockSpec(memory_space=pltpu.VMEM),
        scratch_shapes=[
            pltpu.VMEM((rows, tiles + 2, xs + 2 * PAD, LANES), jnp.float32),
            pltpu.VMEM((7, tiles_per, UNIT, LANES), jnp.float32),
            pltpu.VMEM((depth_n - 1, pairs, 7, UNIT, cols), jnp.bfloat16),
            pltpu.VMEM((depth_n, pairs, 7, UNIT, cols), jnp.bfloat16),
            pltpu.SemaphoreType.DMA((tiles,)),
            pltpu.SemaphoreType.DMA((2, tiles)),
            pltpu.SemaphoreType.DMA((2, tiles)),
            pltpu.SemaphoreType.DMA((depth_n - 1, pairs)),
            pltpu.SemaphoreType.DMA((depth_n, pairs)),
        ],
        compiler_params=pltpu.CompilerParams(
            collective_id=0, has_side_effects=True, vmem_limit_bytes=64 * 1024 * 1024
        ),
        name="render",
    )(density, palette, light_dir, slab_of)


def solution(mesh):
    in_specs = (P("depth", "tile", None), P(), P(), P())
    out_specs = P(None, None, "tile", "depth")
    body = functools.partial(on_device, mesh.shape["depth"], mesh.shape["tile"])
    return jax.shard_map(
        body, mesh=mesh, in_specs=in_specs, out_specs=out_specs, check_vma=False
    )
```

```python
import functools
import math

import jax
import jax.numpy as jnp
from jax import lax
from jax.experimental import pallas as pl
from jax.experimental.pallas import tpu as pltpu
from jax.sharding import PartitionSpec as P

LANES = 128
SUB = 8
UNIT = 16
PAD = 8


def partner(me, step, count):
    if count & (count - 1):
        return lax.rem(me + step, count)
    out, bit = 0, 1
    while bit < count:
        mine = lax.rem(me // bit, 2)
        out = out + bit * (1 - mine if step & bit else mine)
        bit *= 2
    return out


def kernel(
    geom, density, planes, palette, light, slab_of, out, buf, stag, send, recv,
    load_sem, halo_send, halo_recv, send_sem, recv_sem,
):
    rows, xs, ncols, depth_n, tile_n, tiles_per, group, unroll = geom
    tiles = ncols // LANES
    me = lax.axis_index("depth")
    tile = lax.axis_index("tile")
    left = lax.rem(tile + tile_n - 1, tile_n)
    right = lax.rem(tile + 1, tile_n)
    barrier = pltpu.get_barrier_semaphore()
    for step in range(1, depth_n):
        pl.semaphore_signal(
            barrier, inc=1, device_id={"depth": partner(me, step, depth_n)},
            device_id_type=pl.DeviceIdType.MESH,
        )
    for side in (left, right):
        pl.semaphore_signal(
            barrier, inc=1, device_id={"tile": side}, device_id_type=pl.DeviceIdType.MESH
        )

    def chunk_of(step):
        return partner(me, step, depth_n) if step else me

    steps = list(range(depth_n - 1, -1, -1))

    def load(step, i):
        chunk = chunk_of(step)
        j = jnp.clip(chunk * tiles_per + i - 1, 0, tiles - 1)
        return pltpu.make_async_copy(
            density.at[:, :, pl.ds(pl.multiple_of(j * LANES, LANES), LANES)],
            buf.at[:, chunk, i, pl.ds(PAD, xs), :],
            load_sem.at[step, i],
        )

    def start_loads(step):
        for i in range(tiles_per + 2):
            load(step, i).start()

    def finish_loads(step):
        for i in range(tiles_per + 2):
            load(step, i).wait()
        chunk = chunk_of(step)

        def pad_columns(z, own, pad, shift):
            for x0 in range(0, xs, SUB):
                here = pl.ds(PAD + x0, SUB)
                buf[z, chunk, pad, here, :] = pltpu.roll(buf[z, chunk, own, here, :], shift, 1)

        @pl.when(chunk == 0)
        def _():
            @pl.loop(0, rows, step=4)
            def _(z):
                for i in range(4):
                    pad_columns(z + i, 1, 0, LANES - 1)

        @pl.when(chunk == depth_n - 1)
        def _():
            @pl.loop(0, rows, step=4)
            def _(z):
                for i in range(4):
                    pad_columns(z + i, tiles_per, tiles_per + 1, 1)

    start_loads(steps[0])
    pl.semaphore_wait(barrier, depth_n + 1)

    low_row, high_row = PAD - 1, PAD + xs

    def halo_part(source, row):
        return (
            planes.at[:, source // SUB, :, :, pl.ds(source % SUB, 1), :],
            buf.at[:, :, pl.ds(1, tiles_per), pl.ds(row, 1), :],
        )

    def halo_to(side):
        src, dst = halo_part(*((xs - 1, low_row), (0, high_row))[side])
        return pltpu.make_async_remote_copy(
            src_ref=src,
            dst_ref=dst,
            send_sem=halo_send.at[side],
            recv_sem=halo_recv.at[side],
            device_id={"tile": (right, left)[side]},
            device_id_type=pl.DeviceIdType.MESH,
        )

    def halo_own(side):
        src, dst = halo_part(*((0, low_row), (xs - 1, high_row))[side])
        return pltpu.make_async_copy(src, dst, halo_recv.at[side])

    for side, (sends, has) in enumerate(
        ((tile < tile_n - 1, tile > 0), (tile > 0, tile < tile_n - 1))
    ):

        @pl.when(sends)
        def _(side=side):
            halo_to(side).start()

        @pl.when(jnp.logical_not(has))
        def _(side=side):
            halo_own(side).start()

    for step in steps[1:]:
        start_loads(step)

    factor = 3.0 / (rows * depth_n)
    scale = factor * math.log2(math.e)
    lights = [[light[v, c] for c in range(3)] for v in range(2)]
    colours = [[palette[a, c] for c in range(3)] for a in range(2)]
    lane = lax.broadcasted_iota(jnp.int32, (group, SUB, LANES), 2)
    first, last = lane == 0, lane == LANES - 1

    def sweep(chunk, j0, x0, stag_j, stag_row):
        here = pl.ds(pl.multiple_of(x0 + PAD, SUB), SUB)

        def at(z, offset=0):
            where = pl.ds(x0 + PAD + offset, SUB) if offset else here
            return buf[z, chunk, pl.ds(j0 + 1, group), where, :]

        def block(step, carry):
            run, seen, grown, p0, d0, p1, d1 = carry
            z0 = step * unroll
            below = at(max(z0 - 1, 0) if unroll == rows else jnp.maximum(z0 - 1, 0))
            mid = at(z0)
            for i in range(unroll):
                z = z0 + i
                if unroll == rows:
                    above = at(min(z + 1, rows - 1))
                else:
                    above = at(jnp.minimum(z + 1, rows - 1) if i == unroll - 1 else z + 1)
                gz = above - below
                gx = at(z, 1) - at(z, -1)
                edge_low = buf[z, chunk, pl.ds(j0, 1), here, :]
                edge_high = buf[z, chunk, pl.ds(j0 + group + 1, 1), here, :]
                if group > 1:
                    edge_low = jnp.concatenate([edge_low, mid[:-1]], 0)
                    edge_high = jnp.concatenate([mid[1:], edge_high], 0)
                prior = pltpu.roll(jnp.where(last, edge_low, mid), 1, 2)
                after = pltpu.roll(jnp.where(first, edge_high, mid), LANES - 1, 2)
                gy = after - prior
                inverse = lax.rsqrt(gx * gx + gy * gy + (gz * gz + 1.0))
                shades = [
                    jnp.abs(gx * l[0] + gy * l[1] + gz * l[2]) * inverse + 0.3 for l in lights
                ]
                run = run + mid
                power = run * scale
                seen_next = jnp.exp2(-power)
                grown_next = jnp.exp2(power)
                c0 = (seen - seen_next) * shades[0]
                c1 = (grown_next - grown) * shades[1]
                p0 = p0 + c0
                d0 = d0 + mid * c0
                p1 = p1 + c1
                d1 = d1 + mid * c1
                seen, grown = seen_next, grown_next
                below, mid = mid, above
            return run, seen, grown, p0, d0, p1, d1

        zero = jnp.zeros((group, SUB, LANES), jnp.float32)
        one = jnp.ones((group, SUB, LANES), jnp.float32)
        carry = (zero, one, one, zero, zero, zero, zero)
        if unroll == rows:
            carry = block(0, carry)
        else:
            carry = lax.fori_loop(0, rows // unroll, block, carry)
        run, seen, _, p0, d0, p1, d1 = carry
        p1, d1 = p1 * seen, d1 * seen
        fields = [colours[0][c] * p0 + colours[1][c] * d0 for c in range(3)]
        fields += [colours[0][c] * p1 + colours[1][c] * d1 for c in range(3)]
        fields.append(run * factor)
        for f, value in enumerate(fields):
            stag[f, pl.ds(stag_j, group), pl.ds(pl.multiple_of(stag_row, SUB), SUB), :] = value

    groups = tiles_per // group

    def unit(dest, x_first, x_step, target):
        def part(index, _):
            half, piece = index // groups, lax.rem(index, groups)
            sweep(
                dest, piece * group, x_first + half * x_step, piece * group, half * SUB
            )
            return 0

        lax.fori_loop(0, 2 * groups, part, 0)
        for f in range(7):
            for j in range(tiles_per):
                target[f, :, pl.ds(j * LANES, LANES)] = stag[f, j].astype(jnp.bfloat16)

    def outgoing(step, u):
        return pltpu.make_async_remote_copy(
            src_ref=send.at[step - 1, u],
            dst_ref=recv.at[me, u],
            send_sem=send_sem.at[step - 1, u],
            recv_sem=recv_sem.at[me, u],
            device_id={"depth": partner(me, step, depth_n)},
            device_id_type=pl.DeviceIdType.MESH,
        )

    def incoming(source, u):
        return pltpu.make_async_remote_copy(
            src_ref=send.at[0, u],
            dst_ref=recv.at[source, u],
            send_sem=send_sem.at[0, u],
            recv_sem=recv_sem.at[source, u],
            device_id={"depth": source},
            device_id_type=pl.DeviceIdType.MESH,
        )

    pairs = xs // UNIT

    def rows_of(u):
        return (0, xs - SUB) if u == pairs - 1 else (SUB + u * UNIT, SUB)

    for u in range(pairs):
        if u == pairs - 1:
            for side, has in ((0, tile > 0), (1, tile < tile_n - 1)):

                @pl.when(has)
                def _(side=side):
                    halo_to(side).wait_recv()

                @pl.when(jnp.logical_not(has))
                def _(side=side):
                    halo_own(side).wait()

        for step in steps[:-1]:
            if u == 0:
                finish_loads(step)
            unit(partner(me, step, depth_n), *rows_of(u), send.at[step - 1, u])
            outgoing(step, u).start()

    finish_loads(0)
    for u in range(pairs):
        unit(me, *rows_of(u), recv.at[me, u])

    order = [slab_of[k] for k in range(depth_n)]
    for u in range(pairs):
        for step in range(1, depth_n):
            incoming(partner(me, step, depth_n), u).wait_recv()
        x_first, x_step = rows_of(u)

        def compose(j, _):
            cols = pl.ds(pl.multiple_of(j * LANES, LANES), LANES)
            taus = [recv[k, u, 6, :, cols].astype(jnp.float32) for k in range(depth_n)]
            total = functools.reduce(jnp.add, taus)
            coverage = 1.0 - jnp.exp(-total)
            sums = [[0.0] * 3 for _ in range(2)]
            for b in range(depth_n):
                front = jnp.zeros_like(total)
                behind = jnp.zeros_like(total)
                for k in range(depth_n):
                    if k != b:
                        front += jnp.where(order[k] < order[b], 1.0, 0.0) * taus[k]
                        behind += jnp.where(order[k] > order[b], 1.0, 0.0) * taus[k]
                for v, depth in enumerate((front, behind)):
                    fade = jnp.exp(-depth)
                    for c in range(3):
                        value = recv[b, u, 3 * v + c, :, cols].astype(jnp.float32)
                        sums[v][c] = sums[v][c] + value * fade
            for v in range(2):
                for c, value in enumerate(sums[v] + [coverage]):
                    for half in range(2):
                        out[v, c, pl.ds(x_first + half * x_step, SUB), cols] = value[
                            half * SUB : (half + 1) * SUB
                        ]
            return 0

        lax.fori_loop(0, tiles_per, compose, 0)

    for u in range(pairs):
        for step in range(1, depth_n):
            outgoing(step, u).wait_send()
    for side, sends in enumerate((tile < tile_n - 1, tile > 0)):

        @pl.when(sends)
        def _(side=side):
            halo_to(side).wait_send()


def on_device(depth_n, tile_n, density, palette, light_dir, slab_of):
    rows, xs, ncols = density.shape
    tiles = ncols // LANES
    tiles_per = tiles // depth_n
    group = 2 if tiles_per % 2 == 0 else 1
    unroll = rows
    geom = (rows, xs, ncols, depth_n, tile_n, tiles_per, group, unroll)
    pairs = xs // UNIT
    cols = ncols // depth_n
    planes = density.reshape(rows, xs // SUB, SUB, depth_n, tiles_per, LANES)
    planes = planes.transpose(0, 1, 3, 4, 2, 5)
    smem = pl.BlockSpec(memory_space=pltpu.SMEM)
    return pl.pallas_call(
        functools.partial(kernel, geom),
        out_shape=jax.ShapeDtypeStruct((2, 4, xs, cols), jnp.float32),
        in_specs=[pl.BlockSpec(memory_space=pl.ANY)] * 2 + [smem, smem, smem],
        out_specs=pl.BlockSpec(memory_space=pltpu.VMEM),
        scratch_shapes=[
            pltpu.VMEM((rows, depth_n, tiles_per + 2, xs + 2 * PAD, LANES), jnp.float32),
            pltpu.VMEM((7, tiles_per, UNIT, LANES), jnp.float32),
            pltpu.VMEM((depth_n - 1, pairs, 7, UNIT, cols), jnp.bfloat16),
            pltpu.VMEM((depth_n, pairs, 7, UNIT, cols), jnp.bfloat16),
            pltpu.SemaphoreType.DMA((depth_n, tiles_per + 2)),
            pltpu.SemaphoreType.DMA((2,)),
            pltpu.SemaphoreType.DMA((2,)),
            pltpu.SemaphoreType.DMA((depth_n - 1, pairs)),
            pltpu.SemaphoreType.DMA((depth_n, pairs)),
        ],
        compiler_params=pltpu.CompilerParams(
            collective_id=0, has_side_effects=True, vmem_limit_bytes=(64 * 1024 - 640) * 1024
        ),
        name="render",
    )(density, planes, palette, light_dir, slab_of)


def solution(mesh):
    in_specs = (P("depth", "tile", None), P(), P(), P())
    out_specs = P(None, None, "tile", "depth")
    body = functools.partial(on_device, mesh.shape["depth"], mesh.shape["tile"])
    return jax.shard_map(
        body, mesh=mesh, in_specs=in_specs, out_specs=out_specs, check_vma=False
    )
```

```python
import functools
import math

import jax
import jax.numpy as jnp
from jax import lax
from jax.experimental import pallas as pl
from jax.experimental.pallas import tpu as pltpu
from jax.sharding import PartitionSpec as P

LANES = 128
SUB = 8
UNIT = 16
PAD = 8


def partner(me, step, count):
    if count & (count - 1):
        return lax.rem(me + step, count)
    out, bit = 0, 1
    while bit < count:
        mine = lax.rem(me // bit, 2)
        flip = lax.rem(step // bit, 2)
        out = out + bit * (mine + flip - 2 * mine * flip)
        bit *= 2
    return out


def kernel(
    geom, density, planes, palette, light, slab_of, out, buf, stag, send, recv,
    load_sem, halo_send, halo_recv, send_sem, recv_sem,
):
    rows, xs, ncols, depth_n, tile_n, tiles_per, group, unroll = geom
    tiles = ncols // LANES
    me = lax.axis_index("depth")
    tile = lax.axis_index("tile")
    left = lax.rem(tile + tile_n - 1, tile_n)
    right = lax.rem(tile + 1, tile_n)
    barrier = pltpu.get_barrier_semaphore()
    for step in range(1, depth_n):
        pl.semaphore_signal(
            barrier, inc=1, device_id={"depth": partner(me, step, depth_n)},
            device_id_type=pl.DeviceIdType.MESH,
        )
    for side in (left, right):
        pl.semaphore_signal(
            barrier, inc=1, device_id={"tile": side}, device_id_type=pl.DeviceIdType.MESH
        )

    def chunk_of(step):
        return partner(me, step, depth_n)

    steps = list(range(depth_n - 1, -1, -1))

    def load(step, i):
        chunk = chunk_of(step)
        j = jnp.clip(chunk * tiles_per + i - 1, 0, tiles - 1)
        return pltpu.make_async_copy(
            density.at[:, :, pl.ds(pl.multiple_of(j * LANES, LANES), LANES)],
            buf.at[:, chunk, i, pl.ds(PAD, xs), :],
            load_sem.at[step, i],
        )

    def start_loads(step):
        for i in range(tiles_per + 2):
            load(step, i).start()

    def finish_loads(step):
        for i in range(tiles_per + 2):
            load(step, i).wait()
        chunk = chunk_of(step)

        def pad_columns(z, own, pad, shift):
            for x0 in range(0, xs, SUB):
                here = pl.ds(PAD + x0, SUB)
                buf[z, chunk, pad, here, :] = pltpu.roll(buf[z, chunk, own, here, :], shift, 1)

        @pl.when(chunk == 0)
        def _():
            @pl.loop(0, rows, step=4)
            def _(z):
                for i in range(4):
                    pad_columns(z + i, 1, 0, LANES - 1)

        @pl.when(chunk == depth_n - 1)
        def _():
            @pl.loop(0, rows, step=4)
            def _(z):
                for i in range(4):
                    pad_columns(z + i, tiles_per, tiles_per + 1, 1)

    start_loads(steps[0])
    pl.semaphore_wait(barrier, depth_n + 1)

    low_row, high_row = PAD - 1, PAD + xs

    def halo_part(source, row):
        return (
            planes.at[:, source // SUB, :, :, pl.ds(source % SUB, 1), :],
            buf.at[:, :, pl.ds(1, tiles_per), pl.ds(row, 1), :],
        )

    def halo_to(side):
        src, dst = halo_part(*((xs - 1, low_row), (0, high_row))[side])
        return pltpu.make_async_remote_copy(
            src_ref=src,
            dst_ref=dst,
            send_sem=halo_send.at[side],
            recv_sem=halo_recv.at[side],
            device_id={"tile": (right, left)[side]},
            device_id_type=pl.DeviceIdType.MESH,
        )

    def halo_own(side):
        src, dst = halo_part(*((0, low_row), (xs - 1, high_row))[side])
        return pltpu.make_async_copy(src, dst, halo_recv.at[side])

    for side, (sends, has) in enumerate(
        ((tile < tile_n - 1, tile > 0), (tile > 0, tile < tile_n - 1))
    ):

        @pl.when(sends)
        def _(side=side):
            halo_to(side).start()

        @pl.when(jnp.logical_not(has))
        def _(side=side):
            halo_own(side).start()

    for step in steps[1:]:
        start_loads(step)

    factor = 3.0 / (rows * depth_n)
    scale = factor * math.log2(math.e)
    lights = [[light[v, c] for c in range(3)] for v in range(2)]
    colours = [[palette[a, c] for c in range(3)] for a in range(2)]
    lane = lax.broadcasted_iota(jnp.int32, (group, SUB, LANES), 2)
    first, last = lane == 0, lane == LANES - 1

    def sweep(chunk, j0, x0, stag_j, stag_row):
        here = pl.ds(pl.multiple_of(x0 + PAD, SUB), SUB)

        def at(z, offset=0):
            where = pl.ds(x0 + PAD + offset, SUB) if offset else here
            return buf[z, chunk, pl.ds(j0 + 1, group), where, :]

        def block(step, carry):
            run, seen, grown, p0, d0, p1, d1 = carry
            z0 = step * unroll
            below = at(max(z0 - 1, 0) if unroll == rows else jnp.maximum(z0 - 1, 0))
            mid = at(z0)
            for i in range(unroll):
                z = z0 + i
                if unroll == rows:
                    above = at(min(z + 1, rows - 1))
                else:
                    above = at(jnp.minimum(z + 1, rows - 1) if i == unroll - 1 else z + 1)
                gz = above - below
                gx = at(z, 1) - at(z, -1)
                edge_low = buf[z, chunk, pl.ds(j0, 1), here, :]
                edge_high = buf[z, chunk, pl.ds(j0 + group + 1, 1), here, :]
                if group > 1:
                    edge_low = jnp.concatenate([edge_low, mid[:-1]], 0)
                    edge_high = jnp.concatenate([mid[1:], edge_high], 0)
                prior = pltpu.roll(jnp.where(last, edge_low, mid), 1, 2)
                after = pltpu.roll(jnp.where(first, edge_high, mid), LANES - 1, 2)
                gy = after - prior
                inverse = lax.rsqrt(gx * gx + gy * gy + (gz * gz + 1.0))
                shades = [
                    jnp.abs(gx * l[0] + gy * l[1] + gz * l[2]) * inverse + 0.3 for l in lights
                ]
                run = run + mid
                power = run * scale
                seen_next = jnp.exp2(-power)
                grown_next = jnp.exp2(power)
                c0 = (seen - seen_next) * shades[0]
                c1 = (grown_next - grown) * shades[1]
                p0 = p0 + c0
                d0 = d0 + mid * c0
                p1 = p1 + c1
                d1 = d1 + mid * c1
                seen, grown = seen_next, grown_next
                below, mid = mid, above
            return run, seen, grown, p0, d0, p1, d1

        zero = jnp.zeros((group, SUB, LANES), jnp.float32)
        one = jnp.ones((group, SUB, LANES), jnp.float32)
        carry = (zero, one, one, zero, zero, zero, zero)
        if unroll == rows:
            carry = block(0, carry)
        else:
            carry = lax.fori_loop(0, rows // unroll, block, carry)
        run, seen, _, p0, d0, p1, d1 = carry
        p1, d1 = p1 * seen, d1 * seen
        fields = [colours[0][c] * p0 + colours[1][c] * d0 for c in range(3)]
        fields += [colours[0][c] * p1 + colours[1][c] * d1 for c in range(3)]
        fields.append(run * factor)
        for f, value in enumerate(fields):
            stag[f, pl.ds(stag_j, group), pl.ds(stag_row, SUB), :] = value

    groups = tiles_per // group

    def store(target):
        for f in range(7):
            for j in range(tiles_per):
                target[f, :, pl.ds(j * LANES, LANES)] = stag[f, j].astype(jnp.bfloat16)

    def outgoing(step, u):
        return pltpu.make_async_remote_copy(
            src_ref=send.at[step - 1, u],
            dst_ref=recv.at[me, u],
            send_sem=send_sem.at[step - 1, u],
            recv_sem=recv_sem.at[me, u],
            device_id={"depth": partner(me, step, depth_n)},
            device_id_type=pl.DeviceIdType.MESH,
        )

    def incoming(source, u):
        return pltpu.make_async_remote_copy(
            src_ref=send.at[0, u],
            dst_ref=recv.at[source, u],
            send_sem=send_sem.at[0, u],
            recv_sem=recv_sem.at[source, u],
            device_id={"depth": source},
            device_id_type=pl.DeviceIdType.MESH,
        )

    pairs = xs // UNIT

    def rows_of(u):
        return (0, xs - SUB) if u == pairs - 1 else (SUB + u * UNIT, SUB)

    remote = pairs * (depth_n - 1)

    def unit(t, _):
        own = t >= remote
        u = jnp.where(own, t - remote, t // (depth_n - 1))
        step = jnp.where(own, 0, depth_n - 1 - lax.rem(t, depth_n - 1))

        @pl.when((t < depth_n - 1) | (t == remote))
        def _():
            finish_loads(step)

        for side, has in ((0, tile > 0), (1, tile < tile_n - 1)):

            @pl.when((t == (pairs - 1) * (depth_n - 1)) & has)
            def _(side=side):
                halo_to(side).wait_recv()

            @pl.when((t == (pairs - 1) * (depth_n - 1)) & jnp.logical_not(has))
            def _(side=side):
                halo_own(side).wait()

        outer = u == pairs - 1
        x_first = jnp.where(outer, 0, SUB + u * UNIT)
        x_step = jnp.where(outer, xs - SUB, SUB)
        dest = chunk_of(step)
        for half in range(2):
            for piece in range(groups):
                sweep(
                    dest, piece * group, x_first + half * x_step, piece * group, half * SUB
                )

        @pl.when(own)
        def _():
            store(recv.at[me, u])

        @pl.when(jnp.logical_not(own))
        def _():
            store(send.at[step - 1, u])
            outgoing(step, u).start()

        return 0

    lax.fori_loop(0, remote + pairs, unit, 0)

    order = [slab_of[k] for k in range(depth_n)]
    for u in range(pairs):
        for step in range(1, depth_n):
            incoming(partner(me, step, depth_n), u).wait_recv()
        x_first, x_step = rows_of(u)

        def compose(j, _):
            cols = pl.ds(pl.multiple_of(j * LANES, LANES), LANES)
            taus = [recv[k, u, 6, :, cols].astype(jnp.float32) for k in range(depth_n)]
            total = functools.reduce(jnp.add, taus)
            coverage = 1.0 - jnp.exp(-total)
            sums = [[0.0] * 3 for _ in range(2)]
            for b in range(depth_n):
                front = jnp.zeros_like(total)
                behind = jnp.zeros_like(total)
                for k in range(depth_n):
                    if k != b:
                        front += jnp.where(order[k] < order[b], 1.0, 0.0) * taus[k]
                        behind += jnp.where(order[k] > order[b], 1.0, 0.0) * taus[k]
                for v, depth in enumerate((front, behind)):
                    fade = jnp.exp(-depth)
                    for c in range(3):
                        value = recv[b, u, 3 * v + c, :, cols].astype(jnp.float32)
                        sums[v][c] = sums[v][c] + value * fade
            for v in range(2):
                for c, value in enumerate(sums[v] + [coverage]):
                    for half in range(2):
                        out[v, c, pl.ds(x_first + half * x_step, SUB), cols] = value[
                            half * SUB : (half + 1) * SUB
                        ]
            return 0

        lax.fori_loop(0, tiles_per, compose, 0)

    for u in range(pairs):
        for step in range(1, depth_n):
            outgoing(step, u).wait_send()
    for side, sends in enumerate((tile < tile_n - 1, tile > 0)):

        @pl.when(sends)
        def _(side=side):
            halo_to(side).wait_send()


def on_device(depth_n, tile_n, density, palette, light_dir, slab_of):
    rows, xs, ncols = density.shape
    tiles = ncols // LANES
    tiles_per = tiles // depth_n
    group = 2 if tiles_per % 2 == 0 else 1
    unroll = rows
    geom = (rows, xs, ncols, depth_n, tile_n, tiles_per, group, unroll)
    pairs = xs // UNIT
    cols = ncols // depth_n
    planes = density.reshape(rows, xs // SUB, SUB, depth_n, tiles_per, LANES)
    planes = planes.transpose(0, 1, 3, 4, 2, 5)
    smem = pl.BlockSpec(memory_space=pltpu.SMEM)
    return pl.pallas_call(
        functools.partial(kernel, geom),
        out_shape=jax.ShapeDtypeStruct((2, 4, xs, cols), jnp.float32),
        in_specs=[pl.BlockSpec(memory_space=pl.ANY)] * 2 + [smem, smem, smem],
        out_specs=pl.BlockSpec(memory_space=pltpu.VMEM),
        scratch_shapes=[
            pltpu.VMEM((rows, depth_n, tiles_per + 2, xs + 2 * PAD, LANES), jnp.float32),
            pltpu.VMEM((7, tiles_per, UNIT, LANES), jnp.float32),
            pltpu.VMEM((depth_n - 1, pairs, 7, UNIT, cols), jnp.bfloat16),
            pltpu.VMEM((depth_n, pairs, 7, UNIT, cols), jnp.bfloat16),
            pltpu.SemaphoreType.DMA((depth_n, tiles_per + 2)),
            pltpu.SemaphoreType.DMA((2,)),
            pltpu.SemaphoreType.DMA((2,)),
            pltpu.SemaphoreType.DMA((depth_n - 1, pairs)),
            pltpu.SemaphoreType.DMA((depth_n, pairs)),
        ],
        compiler_params=pltpu.CompilerParams(
            collective_id=0, has_side_effects=True, vmem_limit_bytes=(64 * 1024 - 640) * 1024
        ),
        name="render",
    )(density, planes, palette, light_dir, slab_of)


def solution(mesh):
    in_specs = (P("depth", "tile", None), P(), P(), P())
    out_specs = P(None, None, "tile", "depth")
    body = functools.partial(on_device, mesh.shape["depth"], mesh.shape["tile"])
    return jax.shard_map(
        body, mesh=mesh, in_specs=in_specs, out_specs=out_specs, check_vma=False
    )
```

```python
import functools
import math

import jax
import jax.numpy as jnp
from jax import lax
from jax.experimental import pallas as pl
from jax.experimental.pallas import tpu as pltpu
from jax.sharding import PartitionSpec as P

LANES = 128
SUB = 8
UNIT = 16
PAD = 8


def partner(me, step, count):
    if count & (count - 1):
        return lax.rem(me + step, count)
    out, bit = 0, 1
    while bit < count:
        mine = lax.rem(me // bit, 2)
        flip = lax.rem(step // bit, 2)
        out = out + bit * (mine + flip - 2 * mine * flip)
        bit *= 2
    return out


def kernel(
    geom, density, planes, palette, light, slab_of, out, buf, stag, send, recv,
    load_sem, halo_send, halo_recv, send_sem, recv_sem,
):
    rows, xs, ncols, depth_n, tile_n, tiles_per, group, unroll = geom
    tiles = ncols // LANES
    me = lax.axis_index("depth")
    tile = lax.axis_index("tile")
    left = lax.rem(tile + tile_n - 1, tile_n)
    right = lax.rem(tile + 1, tile_n)
    barrier = pltpu.get_barrier_semaphore()
    for step in range(1, depth_n):
        pl.semaphore_signal(
            barrier, inc=1, device_id={"depth": partner(me, step, depth_n)},
            device_id_type=pl.DeviceIdType.MESH,
        )
    for side in (left, right):
        pl.semaphore_signal(
            barrier, inc=1, device_id={"tile": side}, device_id_type=pl.DeviceIdType.MESH
        )

    def chunk_of(step):
        return partner(me, step, depth_n)

    steps = list(range(depth_n - 1, -1, -1))

    def load(step, i):
        chunk = chunk_of(step)
        j = jnp.clip(chunk * tiles_per + i - 1, 0, tiles - 1)
        return pltpu.make_async_copy(
            density.at[:, :, pl.ds(pl.multiple_of(j * LANES, LANES), LANES)],
            buf.at[:, chunk, i, pl.ds(PAD, xs), :],
            load_sem.at[step, i],
        )

    def start_loads(step):
        for i in range(tiles_per + 2):
            load(step, i).start()

    def finish_loads(step):
        for i in range(tiles_per + 2):
            load(step, i).wait()
        chunk = chunk_of(step)

        def pad_columns(z, own, pad, shift):
            for x0 in range(0, xs, SUB):
                here = pl.ds(PAD + x0, SUB)
                buf[z, chunk, pad, here, :] = pltpu.roll(buf[z, chunk, own, here, :], shift, 1)

        @pl.when(chunk == 0)
        def _():
            @pl.loop(0, rows, step=4)
            def _(z):
                for i in range(4):
                    pad_columns(z + i, 1, 0, LANES - 1)

        @pl.when(chunk == depth_n - 1)
        def _():
            @pl.loop(0, rows, step=4)
            def _(z):
                for i in range(4):
                    pad_columns(z + i, tiles_per, tiles_per + 1, 1)

    for step in steps:
        start_loads(step)

    low_row, high_row = PAD - 1, PAD + xs

    def halo_part(source, row):
        return (
            planes.at[:, source // SUB, :, :, pl.ds(source % SUB, 1), :],
            buf.at[:, :, pl.ds(1, tiles_per), pl.ds(row, 1), :],
        )

    def halo_to(side):
        src, dst = halo_part(*((xs - 1, low_row), (0, high_row))[side])
        return pltpu.make_async_remote_copy(
            src_ref=src,
            dst_ref=dst,
            send_sem=halo_send.at[side],
            recv_sem=halo_recv.at[side],
            device_id={"tile": (right, left)[side]},
            device_id_type=pl.DeviceIdType.MESH,
        )

    def halo_own(side):
        src, dst = halo_part(*((0, low_row), (xs - 1, high_row))[side])
        return pltpu.make_async_copy(src, dst, halo_recv.at[side])

    def start_halo():
        for side, (sends, has) in enumerate(
            ((tile < tile_n - 1, tile > 0), (tile > 0, tile < tile_n - 1))
        ):

            @pl.when(sends)
            def _(side=side):
                halo_to(side).start()

            @pl.when(jnp.logical_not(has))
            def _(side=side):
                halo_own(side).start()

    factor = 3.0 / (rows * depth_n)
    scale = factor * math.log2(math.e)
    lights = [[light[v, c] for c in range(3)] for v in range(2)]
    colours = [[palette[a, c] for c in range(3)] for a in range(2)]
    lane = lax.broadcasted_iota(jnp.int32, (group, SUB, LANES), 2)
    first, last = lane == 0, lane == LANES - 1

    def sweep(chunk, j0, x0, stag_j, stag_row):
        here = pl.ds(pl.multiple_of(x0 + PAD, SUB), SUB)

        def at(z, offset=0):
            where = pl.ds(x0 + PAD + offset, SUB) if offset else here
            return buf[z, chunk, pl.ds(j0 + 1, group), where, :]

        def block(step, carry):
            run, seen, grown, p0, d0, p1, d1 = carry
            z0 = step * unroll
            below = at(max(z0 - 1, 0) if unroll == rows else jnp.maximum(z0 - 1, 0))
            mid = at(z0)
            for i in range(unroll):
                z = z0 + i
                if unroll == rows:
                    above = at(min(z + 1, rows - 1))
                else:
                    above = at(jnp.minimum(z + 1, rows - 1) if i == unroll - 1 else z + 1)
                gz = above - below
                gx = at(z, 1) - at(z, -1)
                edge_low = buf[z, chunk, pl.ds(j0, 1), here, :]
                edge_high = buf[z, chunk, pl.ds(j0 + group + 1, 1), here, :]
                if group > 1:
                    edge_low = jnp.concatenate([edge_low, mid[:-1]], 0)
                    edge_high = jnp.concatenate([mid[1:], edge_high], 0)
                prior = pltpu.roll(jnp.where(last, edge_low, mid), 1, 2)
                after = pltpu.roll(jnp.where(first, edge_high, mid), LANES - 1, 2)
                gy = after - prior
                inverse = lax.rsqrt(gx * gx + gy * gy + (gz * gz + 1.0))
                shades = [
                    jnp.abs(gx * l[0] + gy * l[1] + gz * l[2]) * inverse + 0.3 for l in lights
                ]
                run = run + mid
                power = run * scale
                seen_next = jnp.exp2(-power)
                grown_next = jnp.exp2(power)
                c0 = (seen - seen_next) * shades[0]
                c1 = (grown_next - grown) * shades[1]
                p0 = p0 + c0
                d0 = d0 + mid * c0
                p1 = p1 + c1
                d1 = d1 + mid * c1
                seen, grown = seen_next, grown_next
                below, mid = mid, above
            return run, seen, grown, p0, d0, p1, d1

        zero = jnp.zeros((group, SUB, LANES), jnp.float32)
        one = jnp.ones((group, SUB, LANES), jnp.float32)
        carry = (zero, one, one, zero, zero, zero, zero)
        if unroll == rows:
            carry = block(0, carry)
        else:
            carry = lax.fori_loop(0, rows // unroll, block, carry)
        run, seen, _, p0, d0, p1, d1 = carry
        p1, d1 = p1 * seen, d1 * seen
        fields = [colours[0][c] * p0 + colours[1][c] * d0 for c in range(3)]
        fields += [colours[0][c] * p1 + colours[1][c] * d1 for c in range(3)]
        fields.append(run * factor)
        for f, value in enumerate(fields):
            stag[f, pl.ds(stag_j, group), pl.ds(stag_row, SUB), :] = value

    groups = tiles_per // group

    def store(target):
        for f in range(7):
            for j in range(tiles_per):
                target[f, :, pl.ds(j * LANES, LANES)] = stag[f, j].astype(jnp.bfloat16)

    def outgoing(step, u):
        return pltpu.make_async_remote_copy(
            src_ref=send.at[step - 1, u],
            dst_ref=recv.at[me, u],
            send_sem=send_sem.at[step - 1, u],
            recv_sem=recv_sem.at[me, u],
            device_id={"depth": partner(me, step, depth_n)},
            device_id_type=pl.DeviceIdType.MESH,
        )

    def incoming(source, u):
        return pltpu.make_async_remote_copy(
            src_ref=send.at[0, u],
            dst_ref=recv.at[source, u],
            send_sem=send_sem.at[0, u],
            recv_sem=recv_sem.at[source, u],
            device_id={"depth": source},
            device_id_type=pl.DeviceIdType.MESH,
        )

    pairs = xs // UNIT

    def rows_of(u):
        return (0, xs - SUB) if u == pairs - 1 else (SUB + u * UNIT, SUB)

    remote = pairs * (depth_n - 1)

    def meet():
        pl.semaphore_wait(barrier, depth_n + 1)
        start_halo()

    if pairs == 1:
        meet()

    def unit(t, _):
        own = t >= remote
        u = jnp.where(own, t - remote, t // (depth_n - 1))
        step = jnp.where(own, 0, depth_n - 1 - lax.rem(t, depth_n - 1))

        @pl.when((t < depth_n - 1) | (t == remote))
        def _():
            finish_loads(step)

        for side, has in ((0, tile > 0), (1, tile < tile_n - 1)):

            @pl.when((t == (pairs - 1) * (depth_n - 1)) & has)
            def _(side=side):
                halo_to(side).wait_recv()

            @pl.when((t == (pairs - 1) * (depth_n - 1)) & jnp.logical_not(has))
            def _(side=side):
                halo_own(side).wait()

        outer = u == pairs - 1
        x_first = jnp.where(outer, 0, SUB + u * UNIT)
        x_step = jnp.where(outer, xs - SUB, SUB)
        dest = chunk_of(step)
        for half in range(2):
            for piece in range(groups):
                sweep(
                    dest, piece * group, x_first + half * x_step, piece * group, half * SUB
                )

        if pairs > 1:
            pl.when(t == 0)(meet)

        @pl.when(own)
        def _():
            store(recv.at[me, u])

        @pl.when(jnp.logical_not(own))
        def _():
            store(send.at[step - 1, u])
            outgoing(step, u).start()

        return 0

    lax.fori_loop(0, remote + pairs, unit, 0)

    order = [slab_of[k] for k in range(depth_n)]
    for u in range(pairs):
        for step in range(1, depth_n):
            incoming(partner(me, step, depth_n), u).wait_recv()
        x_first, x_step = rows_of(u)

        def compose(j, _):
            cols = pl.ds(pl.multiple_of(j * LANES, LANES), LANES)
            taus = [recv[k, u, 6, :, cols].astype(jnp.float32) for k in range(depth_n)]
            total = functools.reduce(jnp.add, taus)
            coverage = 1.0 - jnp.exp(-total)
            sums = [[0.0] * 3 for _ in range(2)]
            for b in range(depth_n):
                front = jnp.zeros_like(total)
                behind = jnp.zeros_like(total)
                for k in range(depth_n):
                    if k != b:
                        front += jnp.where(order[k] < order[b], 1.0, 0.0) * taus[k]
                        behind += jnp.where(order[k] > order[b], 1.0, 0.0) * taus[k]
                for v, depth in enumerate((front, behind)):
                    fade = jnp.exp(-depth)
                    for c in range(3):
                        value = recv[b, u, 3 * v + c, :, cols].astype(jnp.float32)
                        sums[v][c] = sums[v][c] + value * fade
            for v in range(2):
                for c, value in enumerate(sums[v] + [coverage]):
                    for half in range(2):
                        out[v, c, pl.ds(x_first + half * x_step, SUB), cols] = value[
                            half * SUB : (half + 1) * SUB
                        ]
            return 0

        lax.fori_loop(0, tiles_per, compose, 0)

    for u in range(pairs):
        for step in range(1, depth_n):
            outgoing(step, u).wait_send()
    for side, sends in enumerate((tile < tile_n - 1, tile > 0)):

        @pl.when(sends)
        def _(side=side):
            halo_to(side).wait_send()


def on_device(depth_n, tile_n, density, palette, light_dir, slab_of):
    rows, xs, ncols = density.shape
    tiles = ncols // LANES
    tiles_per = tiles // depth_n
    group = 2 if tiles_per % 2 == 0 else 1
    unroll = rows
    geom = (rows, xs, ncols, depth_n, tile_n, tiles_per, group, unroll)
    pairs = xs // UNIT
    cols = ncols // depth_n
    planes = density.reshape(rows, xs // SUB, SUB, depth_n, tiles_per, LANES)
    planes = planes.transpose(0, 1, 3, 4, 2, 5)
    smem = pl.BlockSpec(memory_space=pltpu.SMEM)
    return pl.pallas_call(
        functools.partial(kernel, geom),
        out_shape=jax.ShapeDtypeStruct((2, 4, xs, cols), jnp.float32),
        in_specs=[pl.BlockSpec(memory_space=pl.ANY)] * 2 + [smem, smem, smem],
        out_specs=pl.BlockSpec(memory_space=pltpu.VMEM),
        scratch_shapes=[
            pltpu.VMEM((rows, depth_n, tiles_per + 2, xs + 2 * PAD, LANES), jnp.float32),
            pltpu.VMEM((7, tiles_per, UNIT, LANES), jnp.float32),
            pltpu.VMEM((depth_n - 1, pairs, 7, UNIT, cols), jnp.bfloat16),
            pltpu.VMEM((depth_n, pairs, 7, UNIT, cols), jnp.bfloat16),
            pltpu.SemaphoreType.DMA((depth_n, tiles_per + 2)),
            pltpu.SemaphoreType.DMA((2,)),
            pltpu.SemaphoreType.DMA((2,)),
            pltpu.SemaphoreType.DMA((depth_n - 1, pairs)),
            pltpu.SemaphoreType.DMA((depth_n, pairs)),
        ],
        compiler_params=pltpu.CompilerParams(
            collective_id=0, has_side_effects=True, vmem_limit_bytes=(64 * 1024 - 640) * 1024
        ),
        name="render",
    )(density, planes, palette, light_dir, slab_of)


def solution(mesh):
    in_specs = (P("depth", "tile", None), P(), P(), P())
    out_specs = P(None, None, "tile", "depth")
    body = functools.partial(on_device, mesh.shape["depth"], mesh.shape["tile"])
    return jax.shard_map(
        body, mesh=mesh, in_specs=in_specs, out_specs=out_specs, check_vma=False
    )
```

```python
import functools
import math

import jax
import jax.numpy as jnp
from jax import lax
from jax.experimental import pallas as pl
from jax.experimental.pallas import tpu as pltpu
from jax.sharding import PartitionSpec as P

LANES = 128
SUB = 8
UNIT = 16
PAD = 8


def partner(me, step, count):
    if count & (count - 1):
        return lax.rem(me + step, count)
    out, bit = 0, 1
    while bit < count:
        mine = lax.rem(me // bit, 2)
        flip = lax.rem(step // bit, 2)
        out = out + bit * (mine + flip - 2 * mine * flip)
        bit *= 2
    return out


def kernel(
    geom, density, planes, palette, light, slab_of, out, buf, stag, send, recv,
    load_sem, halo_send, halo_recv, send_sem, recv_sem,
):
    rows, xs, ncols, depth_n, tile_n, tiles_per, group, unroll = geom
    tiles = ncols // LANES
    me = lax.axis_index("depth")
    tile = lax.axis_index("tile")
    left = lax.rem(tile + tile_n - 1, tile_n)
    right = lax.rem(tile + 1, tile_n)
    barrier = pltpu.get_barrier_semaphore()
    for step in range(1, depth_n):
        pl.semaphore_signal(
            barrier, inc=1, device_id={"depth": partner(me, step, depth_n)},
            device_id_type=pl.DeviceIdType.MESH,
        )
    for side in (left, right):
        pl.semaphore_signal(
            barrier, inc=1, device_id={"tile": side}, device_id_type=pl.DeviceIdType.MESH
        )

    def chunk_of(step):
        return partner(me, step, depth_n)

    steps = list(range(depth_n - 1, -1, -1))

    def load(step, i):
        chunk = chunk_of(step)
        j = jnp.clip(chunk * tiles_per + i - 1, 0, tiles - 1)
        return pltpu.make_async_copy(
            density.at[:, :, pl.ds(pl.multiple_of(j * LANES, LANES), LANES)],
            buf.at[:, chunk, i, pl.ds(PAD, xs), :],
            load_sem.at[step, i],
        )

    def start_loads(step):
        for i in range(tiles_per + 2):
            load(step, i).start()

    def finish_loads(step):
        for i in range(tiles_per + 2):
            load(step, i).wait()
        chunk = chunk_of(step)

        def pad_columns(z, own, pad, shift):
            for x0 in range(0, xs, SUB):
                here = pl.ds(PAD + x0, SUB)
                buf[z, chunk, pad, here, :] = pltpu.roll(buf[z, chunk, own, here, :], shift, 1)

        @pl.when(chunk == 0)
        def _():
            @pl.loop(0, rows, step=4)
            def _(z):
                for i in range(4):
                    pad_columns(z + i, 1, 0, LANES - 1)

        @pl.when(chunk == depth_n - 1)
        def _():
            @pl.loop(0, rows, step=4)
            def _(z):
                for i in range(4):
                    pad_columns(z + i, tiles_per, tiles_per + 1, 1)

    for step in steps:
        start_loads(step)

    low_row, high_row = PAD - 1, PAD + xs

    def halo_part(source, row):
        return (
            planes.at[:, source // SUB, :, :, pl.ds(source % SUB, 1), :],
            buf.at[:, :, pl.ds(1, tiles_per), pl.ds(row, 1), :],
        )

    def halo_to(side):
        src, dst = halo_part(*((xs - 1, low_row), (0, high_row))[side])
        return pltpu.make_async_remote_copy(
            src_ref=src,
            dst_ref=dst,
            send_sem=halo_send.at[side],
            recv_sem=halo_recv.at[side],
            device_id={"tile": (right, left)[side]},
            device_id_type=pl.DeviceIdType.MESH,
        )

    def halo_own(side):
        src, dst = halo_part(*((0, low_row), (xs - 1, high_row))[side])
        return pltpu.make_async_copy(src, dst, halo_recv.at[side])

    def start_halo():
        for side, (sends, has) in enumerate(
            ((tile < tile_n - 1, tile > 0), (tile > 0, tile < tile_n - 1))
        ):

            @pl.when(sends)
            def _(side=side):
                halo_to(side).start()

            @pl.when(jnp.logical_not(has))
            def _(side=side):
                halo_own(side).start()

    factor = 3.0 / (rows * depth_n)
    scale = factor * math.log2(math.e)
    lights = [[light[v, c] for c in range(3)] for v in range(2)]
    colours = [[palette[a, c] for c in range(3)] for a in range(2)]
    lane = lax.broadcasted_iota(jnp.int32, (group, SUB, LANES), 2)
    first, last = lane == 0, lane == LANES - 1

    def sweep(chunk, j0, x0, stag_j, stag_row):
        here = pl.ds(pl.multiple_of(x0 + PAD, SUB), SUB)

        def at(z, offset=0):
            where = pl.ds(x0 + PAD + offset, SUB) if offset else here
            return buf[z, chunk, pl.ds(j0 + 1, group), where, :]

        def block(step, carry):
            run, seen, p0, d0, p1, d1 = carry
            z0 = step * unroll
            below = at(max(z0 - 1, 0) if unroll == rows else jnp.maximum(z0 - 1, 0))
            mid = at(z0)
            for i in range(unroll):
                z = z0 + i
                if unroll == rows:
                    above = at(min(z + 1, rows - 1))
                else:
                    above = at(jnp.minimum(z + 1, rows - 1) if i == unroll - 1 else z + 1)
                gz = above - below
                gx = at(z, 1) - at(z, -1)
                edge_low = buf[z, chunk, pl.ds(j0, 1), here, :]
                edge_high = buf[z, chunk, pl.ds(j0 + group + 1, 1), here, :]
                if group > 1:
                    edge_low = jnp.concatenate([edge_low, mid[:-1]], 0)
                    edge_high = jnp.concatenate([mid[1:], edge_high], 0)
                prior = pltpu.roll(jnp.where(last, edge_low, mid), 1, 2)
                after = pltpu.roll(jnp.where(first, edge_high, mid), LANES - 1, 2)
                gy = after - prior
                inverse = lax.rsqrt(gx * gx + gy * gy + (gz * gz + 1.0))
                shades = [
                    jnp.abs(gx * l[0] + gy * l[1] + gz * l[2]) * inverse + 0.3 for l in lights
                ]
                run = run + mid
                passed = jnp.exp2(mid * -scale)
                opacity = 1.0 - passed
                taken = seen * opacity
                seen = seen - taken
                c0 = taken * shades[0]
                c1 = opacity * shades[1]
                p0 = p0 + c0
                d0 = d0 + mid * c0
                p1 = p1 * passed + c1
                d1 = d1 * passed + mid * c1
                below, mid = mid, above
            return run, seen, p0, d0, p1, d1

        zero = jnp.zeros((group, SUB, LANES), jnp.float32)
        one = jnp.ones((group, SUB, LANES), jnp.float32)
        carry = (zero, one, zero, zero, zero, zero)
        if unroll == rows:
            carry = block(0, carry)
        else:
            carry = lax.fori_loop(0, rows // unroll, block, carry)
        run, seen, p0, d0, p1, d1 = carry
        fields = [colours[0][c] * p0 + colours[1][c] * d0 for c in range(3)]
        fields += [colours[0][c] * p1 + colours[1][c] * d1 for c in range(3)]
        fields.append(run * factor)
        for f, value in enumerate(fields):
            stag[f, pl.ds(stag_j, group), pl.ds(stag_row, SUB), :] = value

    groups = tiles_per // group

    def store(target):
        for f in range(7):
            for j in range(tiles_per):
                target[f, :, pl.ds(j * LANES, LANES)] = stag[f, j].astype(jnp.bfloat16)

    def outgoing(step, u):
        return pltpu.make_async_remote_copy(
            src_ref=send.at[step - 1, u],
            dst_ref=recv.at[me, u],
            send_sem=send_sem.at[step - 1, u],
            recv_sem=recv_sem.at[me, u],
            device_id={"depth": partner(me, step, depth_n)},
            device_id_type=pl.DeviceIdType.MESH,
        )

    def incoming(source, u):
        return pltpu.make_async_remote_copy(
            src_ref=send.at[0, u],
            dst_ref=recv.at[source, u],
            send_sem=send_sem.at[0, u],
            recv_sem=recv_sem.at[source, u],
            device_id={"depth": source},
            device_id_type=pl.DeviceIdType.MESH,
        )

    pairs = xs // UNIT

    def rows_of(u):
        return (0, xs - SUB) if u == pairs - 1 else (SUB + u * UNIT, SUB)

    remote = pairs * (depth_n - 1)

    def meet():
        pl.semaphore_wait(barrier, depth_n + 1)
        start_halo()

    if pairs == 1:
        meet()

    def unit(t, _):
        own = t >= remote
        u = jnp.where(own, t - remote, t // (depth_n - 1))
        step = jnp.where(own, 0, depth_n - 1 - lax.rem(t, depth_n - 1))

        @pl.when((t < depth_n - 1) | (t == remote))
        def _():
            finish_loads(step)

        for side, has in ((0, tile > 0), (1, tile < tile_n - 1)):

            @pl.when((t == (pairs - 1) * (depth_n - 1)) & has)
            def _(side=side):
                halo_to(side).wait_recv()

            @pl.when((t == (pairs - 1) * (depth_n - 1)) & jnp.logical_not(has))
            def _(side=side):
                halo_own(side).wait()

        outer = u == pairs - 1
        x_first = jnp.where(outer, 0, SUB + u * UNIT)
        x_step = jnp.where(outer, xs - SUB, SUB)
        dest = chunk_of(step)
        for half in range(2):
            for piece in range(groups):
                sweep(
                    dest, piece * group, x_first + half * x_step, piece * group, half * SUB
                )

        if pairs > 1:
            pl.when(t == 0)(meet)

        @pl.when(own)
        def _():
            store(recv.at[me, u])

        @pl.when(jnp.logical_not(own))
        def _():
            store(send.at[step - 1, u])
            outgoing(step, u).start()

        return 0

    lax.fori_loop(0, remote + pairs, unit, 0)

    order = [slab_of[k] for k in range(depth_n)]
    for u in range(pairs):
        for step in range(1, depth_n):
            incoming(partner(me, step, depth_n), u).wait_recv()
        x_first, x_step = rows_of(u)

        def compose(j, _):
            cols = pl.ds(pl.multiple_of(j * LANES, LANES), LANES)
            taus = [recv[k, u, 6, :, cols].astype(jnp.float32) for k in range(depth_n)]
            total = functools.reduce(jnp.add, taus)
            coverage = 1.0 - jnp.exp(-total)
            sums = [[0.0] * 3 for _ in range(2)]
            for b in range(depth_n):
                front = jnp.zeros_like(total)
                behind = jnp.zeros_like(total)
                for k in range(depth_n):
                    if k != b:
                        front += jnp.where(order[k] < order[b], 1.0, 0.0) * taus[k]
                        behind += jnp.where(order[k] > order[b], 1.0, 0.0) * taus[k]
                for v, depth in enumerate((front, behind)):
                    fade = jnp.exp(-depth)
                    for c in range(3):
                        value = recv[b, u, 3 * v + c, :, cols].astype(jnp.float32)
                        sums[v][c] = sums[v][c] + value * fade
            for v in range(2):
                for c, value in enumerate(sums[v] + [coverage]):
                    for half in range(2):
                        out[v, c, pl.ds(x_first + half * x_step, SUB), cols] = value[
                            half * SUB : (half + 1) * SUB
                        ]
            return 0

        lax.fori_loop(0, tiles_per, compose, 0)

    for u in range(pairs):
        for step in range(1, depth_n):
            outgoing(step, u).wait_send()
    for side, sends in enumerate((tile < tile_n - 1, tile > 0)):

        @pl.when(sends)
        def _(side=side):
            halo_to(side).wait_send()


def on_device(depth_n, tile_n, density, palette, light_dir, slab_of):
    rows, xs, ncols = density.shape
    tiles = ncols // LANES
    tiles_per = tiles // depth_n
    group = 2 if tiles_per % 2 == 0 else 1
    unroll = rows
    geom = (rows, xs, ncols, depth_n, tile_n, tiles_per, group, unroll)
    pairs = xs // UNIT
    cols = ncols // depth_n
    planes = density.reshape(rows, xs // SUB, SUB, depth_n, tiles_per, LANES)
    planes = planes.transpose(0, 1, 3, 4, 2, 5)
    smem = pl.BlockSpec(memory_space=pltpu.SMEM)
    return pl.pallas_call(
        functools.partial(kernel, geom),
        out_shape=jax.ShapeDtypeStruct((2, 4, xs, cols), jnp.float32),
        in_specs=[pl.BlockSpec(memory_space=pl.ANY)] * 2 + [smem, smem, smem],
        out_specs=pl.BlockSpec(memory_space=pltpu.VMEM),
        scratch_shapes=[
            pltpu.VMEM((rows, depth_n, tiles_per + 2, xs + 2 * PAD, LANES), jnp.float32),
            pltpu.VMEM((7, tiles_per, UNIT, LANES), jnp.float32),
            pltpu.VMEM((depth_n - 1, pairs, 7, UNIT, cols), jnp.bfloat16),
            pltpu.VMEM((depth_n, pairs, 7, UNIT, cols), jnp.bfloat16),
            pltpu.SemaphoreType.DMA((depth_n, tiles_per + 2)),
            pltpu.SemaphoreType.DMA((2,)),
            pltpu.SemaphoreType.DMA((2,)),
            pltpu.SemaphoreType.DMA((depth_n - 1, pairs)),
            pltpu.SemaphoreType.DMA((depth_n, pairs)),
        ],
        compiler_params=pltpu.CompilerParams(
            collective_id=0, has_side_effects=True, vmem_limit_bytes=(64 * 1024 - 640) * 1024
        ),
        name="render",
    )(density, planes, palette, light_dir, slab_of)


def solution(mesh):
    in_specs = (P("depth", "tile", None), P(), P(), P())
    out_specs = P(None, None, "tile", "depth")
    body = functools.partial(on_device, mesh.shape["depth"], mesh.shape["tile"])
    return jax.shard_map(
        body, mesh=mesh, in_specs=in_specs, out_specs=out_specs, check_vma=False
    )
```

```python
import functools
import math

import jax
import jax.numpy as jnp
from jax import lax
from jax.experimental import pallas as pl
from jax.experimental.pallas import tpu as pltpu
from jax.sharding import PartitionSpec as P

LANES = 128
SUB = 8
UNIT = 16
PAD = 8


def partner(me, step, count):
    if count & (count - 1):
        return lax.rem(me + step, count)
    out, bit = 0, 1
    while bit < count:
        mine = lax.rem(me // bit, 2)
        flip = lax.rem(step // bit, 2)
        out = out + bit * (mine + flip - 2 * mine * flip)
        bit *= 2
    return out


def kernel(
    geom, density, planes, palette, light, slab_of, out, buf, stag, send, recv,
    load_sem, halo_send, halo_recv, send_sem, recv_sem,
):
    rows, xs, ncols, depth_n, tile_n, tiles_per, group, unroll = geom
    tiles = ncols // LANES
    me = lax.axis_index("depth")
    tile = lax.axis_index("tile")
    left = lax.rem(tile + tile_n - 1, tile_n)
    right = lax.rem(tile + 1, tile_n)
    barrier = pltpu.get_barrier_semaphore()
    for step in range(1, depth_n):
        pl.semaphore_signal(
            barrier, inc=1, device_id={"depth": partner(me, step, depth_n)},
            device_id_type=pl.DeviceIdType.MESH,
        )
    for side in (left, right):
        pl.semaphore_signal(
            barrier, inc=1, device_id={"tile": side}, device_id_type=pl.DeviceIdType.MESH
        )

    def chunk_of(step):
        return partner(me, step, depth_n)

    steps = list(range(depth_n - 1, -1, -1))

    def load(step, i):
        chunk = chunk_of(step)
        j = jnp.clip(chunk * tiles_per + i - 1, 0, tiles - 1)
        return pltpu.make_async_copy(
            density.at[:, :, pl.ds(pl.multiple_of(j * LANES, LANES), LANES)],
            buf.at[:, chunk, i, pl.ds(PAD, xs), :],
            load_sem.at[step, i],
        )

    def start_loads(step):
        for i in range(tiles_per + 2):
            load(step, i).start()

    def finish_loads(step):
        for i in range(tiles_per + 2):
            load(step, i).wait()
        chunk = chunk_of(step)

        def pad_columns(z, own, pad, shift):
            for x0 in range(0, xs, SUB):
                here = pl.ds(PAD + x0, SUB)
                buf[z, chunk, pad, here, :] = pltpu.roll(buf[z, chunk, own, here, :], shift, 1)

        @pl.when(chunk == 0)
        def _():
            @pl.loop(0, rows, step=4)
            def _(z):
                for i in range(4):
                    pad_columns(z + i, 1, 0, LANES - 1)

        @pl.when(chunk == depth_n - 1)
        def _():
            @pl.loop(0, rows, step=4)
            def _(z):
                for i in range(4):
                    pad_columns(z + i, tiles_per, tiles_per + 1, 1)

    start_loads(steps[0])

    low_row, high_row = PAD - 1, PAD + xs

    def halo_part(source, row):
        return (
            planes.at[:, source // SUB, :, :, pl.ds(source % SUB, 1), :],
            buf.at[:, :, pl.ds(1, tiles_per), pl.ds(row, 1), :],
        )

    def halo_to(side):
        src, dst = halo_part(*((xs - 1, low_row), (0, high_row))[side])
        return pltpu.make_async_remote_copy(
            src_ref=src,
            dst_ref=dst,
            send_sem=halo_send.at[side],
            recv_sem=halo_recv.at[side],
            device_id={"tile": (right, left)[side]},
            device_id_type=pl.DeviceIdType.MESH,
        )

    def halo_own(side):
        src, dst = halo_part(*((0, low_row), (xs - 1, high_row))[side])
        return pltpu.make_async_copy(src, dst, halo_recv.at[side])

    def start_halo():
        for side, (sends, has) in enumerate(
            ((tile < tile_n - 1, tile > 0), (tile > 0, tile < tile_n - 1))
        ):

            @pl.when(sends)
            def _(side=side):
                halo_to(side).start()

            @pl.when(jnp.logical_not(has))
            def _(side=side):
                halo_own(side).start()

    factor = 3.0 / (rows * depth_n)
    scale = factor * math.log2(math.e)
    lights = [[light[v, c] for c in range(3)] for v in range(2)]
    colours = [[palette[a, c] for c in range(3)] for a in range(2)]
    lane = lax.broadcasted_iota(jnp.int32, (group, SUB, LANES), 2)
    first, last = lane == 0, lane == LANES - 1

    def sweep(chunk, j0, x0, stag_j, stag_row):
        here = pl.ds(pl.multiple_of(x0 + PAD, SUB), SUB)

        def at(z, offset=0):
            where = pl.ds(x0 + PAD + offset, SUB) if offset else here
            return buf[z, chunk, pl.ds(j0 + 1, group), where, :]

        def block(step, carry):
            run, seen, grown, p0, d0, p1, d1 = carry
            z0 = step * unroll
            below = at(max(z0 - 1, 0) if unroll == rows else jnp.maximum(z0 - 1, 0))
            mid = at(z0)
            for i in range(unroll):
                z = z0 + i
                if unroll == rows:
                    above = at(min(z + 1, rows - 1))
                else:
                    above = at(jnp.minimum(z + 1, rows - 1) if i == unroll - 1 else z + 1)
                gz = above - below
                gx = at(z, 1) - at(z, -1)
                edge_low = buf[z, chunk, pl.ds(j0, 1), here, :]
                edge_high = buf[z, chunk, pl.ds(j0 + group + 1, 1), here, :]
                if group > 1:
                    edge_low = jnp.concatenate([edge_low, mid[:-1]], 0)
                    edge_high = jnp.concatenate([mid[1:], edge_high], 0)
                prior = pltpu.roll(jnp.where(last, edge_low, mid), 1, 2)
                after = pltpu.roll(jnp.where(first, edge_high, mid), LANES - 1, 2)
                gy = after - prior
                inverse = lax.rsqrt(gx * gx + gy * gy + (gz * gz + 1.0))
                shades = [
                    jnp.abs(gx * l[0] + gy * l[1] + gz * l[2]) * inverse + 0.3 for l in lights
                ]
                run = run + mid
                power = run * scale
                seen_next = jnp.exp2(-power)
                grown_next = jnp.exp2(power)
                c0 = (seen - seen_next) * shades[0]
                c1 = (grown_next - grown) * shades[1]
                p0 = p0 + c0
                d0 = d0 + mid * c0
                p1 = p1 + c1
                d1 = d1 + mid * c1
                seen, grown = seen_next, grown_next
                below, mid = mid, above
            return run, seen, grown, p0, d0, p1, d1

        zero = jnp.zeros((group, SUB, LANES), jnp.float32)
        one = jnp.ones((group, SUB, LANES), jnp.float32)
        carry = (zero, one, one, zero, zero, zero, zero)
        if unroll == rows:
            carry = block(0, carry)
        else:
            carry = lax.fori_loop(0, rows // unroll, block, carry)
        run, seen, _, p0, d0, p1, d1 = carry
        p1, d1 = p1 * seen, d1 * seen
        fields = [colours[0][c] * p0 + colours[1][c] * d0 for c in range(3)]
        fields += [colours[0][c] * p1 + colours[1][c] * d1 for c in range(3)]
        fields.append(run * factor)
        for f, value in enumerate(fields):
            stag[f, pl.ds(stag_j, group), pl.ds(stag_row, SUB), :] = value

    groups = tiles_per // group

    def store(target):
        for f in range(7):
            for j in range(tiles_per):
                target[f, :, pl.ds(j * LANES, LANES)] = stag[f, j].astype(jnp.bfloat16)

    def outgoing(step, u):
        return pltpu.make_async_remote_copy(
            src_ref=send.at[step - 1, u],
            dst_ref=recv.at[me, u],
            send_sem=send_sem.at[step - 1, u],
            recv_sem=recv_sem.at[me, u],
            device_id={"depth": partner(me, step, depth_n)},
            device_id_type=pl.DeviceIdType.MESH,
        )

    def incoming(source, u):
        return pltpu.make_async_remote_copy(
            src_ref=send.at[0, u],
            dst_ref=recv.at[source, u],
            send_sem=send_sem.at[0, u],
            recv_sem=recv_sem.at[source, u],
            device_id={"depth": source},
            device_id_type=pl.DeviceIdType.MESH,
        )

    pairs = xs // UNIT

    def rows_of(u):
        return (0, xs - SUB) if u == pairs - 1 else (SUB + u * UNIT, SUB)

    remote = pairs * (depth_n - 1)

    def meet():
        pl.semaphore_wait(barrier, depth_n + 1)
        start_halo()

    if pairs == 1:
        meet()

    def unit(t, _):
        own = t >= remote
        u = jnp.where(own, t - remote, t // (depth_n - 1))
        step = jnp.where(own, 0, depth_n - 1 - lax.rem(t, depth_n - 1))

        @pl.when((t < depth_n - 1) | (t == remote))
        def _():
            finish_loads(step)

        @pl.when(t == 0)
        def _():
            for later in steps[1:]:
                start_loads(later)

        for side, has in ((0, tile > 0), (1, tile < tile_n - 1)):

            @pl.when((t == (pairs - 1) * (depth_n - 1)) & has)
            def _(side=side):
                halo_to(side).wait_recv()

            @pl.when((t == (pairs - 1) * (depth_n - 1)) & jnp.logical_not(has))
            def _(side=side):
                halo_own(side).wait()

        outer = u == pairs - 1
        x_first = jnp.where(outer, 0, SUB + u * UNIT)
        x_step = jnp.where(outer, xs - SUB, SUB)
        dest = chunk_of(step)
        for half in range(2):
            for piece in range(groups):
                sweep(
                    dest, piece * group, x_first + half * x_step, piece * group, half * SUB
                )

        if pairs > 1:
            pl.when(t == 0)(meet)

        @pl.when(own)
        def _():
            store(recv.at[me, u])

        @pl.when(jnp.logical_not(own))
        def _():
            store(send.at[step - 1, u])
            outgoing(step, u).start()

        return 0

    lax.fori_loop(0, remote + pairs, unit, 0)

    order = [slab_of[k] for k in range(depth_n)]
    for u in range(pairs):
        for step in range(1, depth_n):
            incoming(partner(me, step, depth_n), u).wait_recv()
        x_first, x_step = rows_of(u)

        def compose(j, _):
            cols = pl.ds(pl.multiple_of(j * LANES, LANES), LANES)
            taus = [recv[k, u, 6, :, cols].astype(jnp.float32) for k in range(depth_n)]
            total = functools.reduce(jnp.add, taus)
            coverage = 1.0 - jnp.exp(-total)
            sums = [[0.0] * 3 for _ in range(2)]
            for b in range(depth_n):
                front = jnp.zeros_like(total)
                behind = jnp.zeros_like(total)
                for k in range(depth_n):
                    if k != b:
                        front += jnp.where(order[k] < order[b], 1.0, 0.0) * taus[k]
                        behind += jnp.where(order[k] > order[b], 1.0, 0.0) * taus[k]
                for v, depth in enumerate((front, behind)):
                    fade = jnp.exp(-depth)
                    for c in range(3):
                        value = recv[b, u, 3 * v + c, :, cols].astype(jnp.float32)
                        sums[v][c] = sums[v][c] + value * fade
            for v in range(2):
                for c, value in enumerate(sums[v] + [coverage]):
                    for half in range(2):
                        out[v, c, pl.ds(x_first + half * x_step, SUB), cols] = value[
                            half * SUB : (half + 1) * SUB
                        ]
            return 0

        lax.fori_loop(0, tiles_per, compose, 0)

    for u in range(pairs):
        for step in range(1, depth_n):
            outgoing(step, u).wait_send()
    for side, sends in enumerate((tile < tile_n - 1, tile > 0)):

        @pl.when(sends)
        def _(side=side):
            halo_to(side).wait_send()


def on_device(depth_n, tile_n, density, palette, light_dir, slab_of):
    rows, xs, ncols = density.shape
    tiles = ncols // LANES
    tiles_per = tiles // depth_n
    group = 2 if tiles_per % 2 == 0 else 1
    unroll = rows
    geom = (rows, xs, ncols, depth_n, tile_n, tiles_per, group, unroll)
    pairs = xs // UNIT
    cols = ncols // depth_n
    planes = density.reshape(rows, xs // SUB, SUB, depth_n, tiles_per, LANES)
    planes = planes.transpose(0, 1, 3, 4, 2, 5)
    smem = pl.BlockSpec(memory_space=pltpu.SMEM)
    return pl.pallas_call(
        functools.partial(kernel, geom),
        out_shape=jax.ShapeDtypeStruct((2, 4, xs, cols), jnp.float32),
        in_specs=[pl.BlockSpec(memory_space=pl.ANY)] * 2 + [smem, smem, smem],
        out_specs=pl.BlockSpec(memory_space=pltpu.VMEM),
        scratch_shapes=[
            pltpu.VMEM((rows, depth_n, tiles_per + 2, xs + 2 * PAD, LANES), jnp.float32),
            pltpu.VMEM((7, tiles_per, UNIT, LANES), jnp.float32),
            pltpu.VMEM((depth_n - 1, pairs, 7, UNIT, cols), jnp.bfloat16),
            pltpu.VMEM((depth_n, pairs, 7, UNIT, cols), jnp.bfloat16),
            pltpu.SemaphoreType.DMA((depth_n, tiles_per + 2)),
            pltpu.SemaphoreType.DMA((2,)),
            pltpu.SemaphoreType.DMA((2,)),
            pltpu.SemaphoreType.DMA((depth_n - 1, pairs)),
            pltpu.SemaphoreType.DMA((depth_n, pairs)),
        ],
        compiler_params=pltpu.CompilerParams(
            collective_id=0, has_side_effects=True, vmem_limit_bytes=(64 * 1024 - 640) * 1024
        ),
        name="render",
    )(density, planes, palette, light_dir, slab_of)


def solution(mesh):
    in_specs = (P("depth", "tile", None), P(), P(), P())
    out_specs = P(None, None, "tile", "depth")
    body = functools.partial(on_device, mesh.shape["depth"], mesh.shape["tile"])
    return jax.shard_map(
        body, mesh=mesh, in_specs=in_specs, out_specs=out_specs, check_vma=False
    )
```
